32 devices in a mesh: dp: 8 (over z, core), frame: 4 (over y, x).
Axes of the slice: x: 2, y: 2, z: 4, core: 2. Of those that a mesh axis runs over, the one named last changes fastest.
Arguments:
- latents: bfloat16 [8, 4, 512, 640], P('dp', 'frame'), may hold values from -6 to 6
- cotangent: bfloat16 [8, 4, 512, 640], P('dp', 'frame'), may hold values from -6 to 6
- timesteps: int32 [8], P('dp'), may hold values from 0 to 999
- spatial_weight: bfloat16 [9, 640, 640], replicated, may hold values from -0.078125 to 0.078125
- temporal_weight: bfloat16 [3, 640, 640], replicated, may hold values from -0.125 to 0.125
Outputs:
- new_spatial: float32 [9, 640, 640], P(None, 'frame')
- new_temporal: float32 [3, 640, 640], P(None, 'frame')
The draws below stay inside these ranges and needn't reach their ends.
All inputs are finite; a program needn't handle non-finite values.
Results may differ from the reference program's by a relative error of at most 0.02.
Values may be sent and summed in bfloat16 or wider, within the bound.
A program may use at most 128 MiB of HBM per device.

```python
import math
import jax
import jax.numpy as jnp
from jax import lax

CHANNELS = 640
WIDTH = 64
SLAB = 8
TSTEPS = 1000
PIXELS = 512
FRAMES = 4
SAMPLES = 8


def with_ends(array, stream_key, least, top_value):
    dims = array.shape
    spot = [jax.random.randint(jax.random.fold_in(stream_key, axis), (), 0, dims[axis]) for axis in range(len(dims))]
    array = array.at[tuple(spot)].set(least)
    longest = dims.index(max(dims))
    spot[longest] = (spot[longest] + 1) % dims[longest]
    return array.at[tuple(spot)].set(top_value)


def levels(own_key, dims, shards, low, top_value):
    gain = 1.0
    for position, parts in shards:
        draws = jax.random.uniform(jax.random.fold_in(jax.random.fold_in(own_key, 6), position), (parts,), jnp.float32, low / len(shards), top_value / len(shards))
        gain = gain * jnp.repeat(jnp.exp(draws), dims[position] // parts).reshape((-1,) + (1,) * (len(dims) - 1 - position))
    return gain


def gaussian(rng, extent, deviation, limit, cuts=(), kind=jnp.bfloat16):
    values = jax.random.normal(rng, extent, jnp.float32) * deviation
    if len(cuts) > 0:
        values = levels(rng, extent, cuts, -0.22, 0.18) * values
    return jnp.clip(values, min=-limit, max=limit).astype(kind)


def setup_inputs(seed: int = 0) -> dict:
    splits = jax.random.split(jax.random.key(seed), 6)
    latents = gaussian(splits[0], (SAMPLES, FRAMES, PIXELS, CHANNELS), 1.0, 6.0, ((0, 8), (1, 4)))
    cotangent = gaussian(splits[1], (SAMPLES, FRAMES, PIXELS, CHANNELS), 1.0, 6.0, ((0, 8), (1, 4)))
    timesteps = with_ends(jax.random.randint(splits[2], (SAMPLES,), 0, TSTEPS), jax.random.fold_in(splits[2], 1), 0, TSTEPS - 1).astype(jnp.int32)
    spatial_weight = gaussian(splits[3], (9, CHANNELS, CHANNELS), (9 * CHANNELS) ** -0.5, 0.078125)
    temporal_weight = gaussian(splits[4], (3, CHANNELS, CHANNELS), (3 * CHANNELS) ** -0.5, 0.125)
    return dict(latents=latents, cotangent=cotangent, timesteps=timesteps, spatial_weight=spatial_weight, temporal_weight=temporal_weight)


def embed(timesteps, channels):
    half_width = channels // 2
    frequencies = jnp.exp(-math.log(10000.0) * jnp.arange(half_width, dtype=jnp.float32) / half_width)
    angles = timesteps.astype(jnp.float32)[:, None] * frequencies[None, :]
    return jnp.concatenate([jnp.sin(angles), jnp.cos(angles)], axis=1)

def unfold(activated, slab_rows, grid_width):
    lead_count, pixels, channels = activated.shape
    grid_cells = activated.reshape(lead_count, slab_rows, grid_width, channels)
    padded = jnp.pad(grid_cells, ((0, 0), (1, 1), (1, 1), (0, 0)))
    pieces = [padded[:, row_off:row_off + slab_rows, col_off:col_off + grid_width, :] for row_off in range(3) for col_off in range(3)]
    return jnp.concatenate(pieces, axis=3).reshape(lead_count, pixels, 9 * channels)

def silu_slope(pre_act):
    logistic = jax.nn.sigmoid(pre_act)
    return logistic * (1.0 + pre_act * (1.0 - logistic))

def clip_factor(squares, channels):
    max_norm = 0.5 * math.sqrt(12.0) * channels
    return jnp.minimum(1.0, max_norm / (jnp.sqrt(squares) + 1e-06))

def reference(latents, cotangent, timesteps, spatial_weight, temporal_weight):
    ws_flat = spatial_weight.reshape(9 * CHANNELS, CHANNELS).astype(jnp.float32)
    wt_full = temporal_weight.astype(jnp.float32)
    shifts = embed(timesteps, CHANNELS)

    def one_sample(totals, inputs):
        sample_x, sample_cot, shift_row = inputs
        activated = jax.nn.silu(sample_x.astype(jnp.float32) + shift_row[None, None, :]).astype(jnp.bfloat16)
        columns = unfold(activated, SLAB, WIDTH).astype(jnp.float32)
        pre_act = jnp.einsum('fpk,kc->fpc', columns, ws_flat)
        gated = jax.nn.silu(pre_act).astype(jnp.bfloat16)
        pad_spec = ((1, 1), (0, 0), (0, 0))
        gated_pad = jnp.pad(gated, pad_spec).astype(jnp.float32)
        cot_pad = jnp.pad(sample_cot, pad_spec).astype(jnp.float32)
        cot_full = sample_cot.astype(jnp.float32)
        temporal_grad = jnp.stack([jnp.einsum('fpc,fpd->cd', gated_pad[offset:offset + FRAMES], cot_full) for offset in range(3)])
        grad_gated = jnp.zeros(pre_act.shape, jnp.float32)
        for offset in range(3):
            grad_gated = grad_gated + jnp.einsum('fpd,cd->fpc', cot_pad[2 - offset:2 - offset + FRAMES], wt_full[offset])
        grad_gated = grad_gated.astype(jnp.bfloat16)
        grad_pre = (grad_gated.astype(jnp.float32) * silu_slope(pre_act)).astype(jnp.bfloat16)
        frame_terms = jnp.einsum('fpk,fpc->fkc', columns, grad_pre.astype(jnp.float32)).astype(jnp.bfloat16)
        frame_terms = lax.optimization_barrier(frame_terms).astype(jnp.float32)
        return ((totals[0] + lax.optimization_barrier(jnp.sum(frame_terms, axis=0)), totals[1] + temporal_grad), None)
    start_totals = (jnp.zeros((9 * CHANNELS, CHANNELS), jnp.float32), jnp.zeros((3, CHANNELS, CHANNELS), jnp.float32))
    grads, unused_out = lax.scan(one_sample, start_totals, (latents, cotangent, shifts))
    spatial_grad = grads[0].reshape(9, CHANNELS, CHANNELS)
    temporal_grad = grads[1]
    squares = jnp.sum(spatial_grad * spatial_grad) + jnp.sum(temporal_grad * temporal_grad)
    factor = clip_factor(squares, CHANNELS)
    return (spatial_weight.astype(jnp.float32) - factor * spatial_grad, temporal_weight.astype(jnp.float32) - factor * temporal_grad)
```

```python
import math

import jax
import jax.numpy as jnp
from jax import lax
from jax.sharding import PartitionSpec as P

WIDTH = 64
SLAB = 8


def embed(timesteps, channels):
    half_width = channels // 2
    frequencies = jnp.exp(
        -math.log(10000.0) * jnp.arange(half_width, dtype=jnp.float32) / half_width
    )
    angles = timesteps.astype(jnp.float32)[:, None] * frequencies[None, :]
    return jnp.concatenate([jnp.sin(angles), jnp.cos(angles)], axis=1)


def unfold(activated, slab_rows, grid_width):
    lead_count, pixels, channels = activated.shape
    grid_cells = activated.reshape(lead_count, slab_rows, grid_width, channels)
    padded = jnp.pad(grid_cells, ((0, 0), (1, 1), (1, 1), (0, 0)))
    pieces = [
        padded[:, row_off : row_off + slab_rows, col_off : col_off + grid_width, :]
        for row_off in range(3)
        for col_off in range(3)
    ]
    return jnp.concatenate(pieces, axis=3).reshape(lead_count, pixels, 9 * channels)


def silu_slope(pre_act):
    logistic = jax.nn.sigmoid(pre_act)
    return logistic * (1.0 + pre_act * (1.0 - logistic))


def clip_factor(squares, channels):
    max_norm = 0.5 * math.sqrt(12.0) * channels
    return jnp.minimum(1.0, max_norm / (jnp.sqrt(squares) + 1e-06))


def exchange(array, axis_name, mask):
    count = lax.axis_size(axis_name)
    return lax.ppermute(array, axis_name, [(i, i ^ mask) for i in range(count)])


def halve(array, dim, axis_name, mask):
    mine = jnp.bitwise_and(lax.axis_index(axis_name) // mask, 1)
    keep = lax.dynamic_index_in_dim(array, mine, dim, keepdims=False)
    send = lax.dynamic_index_in_dim(array, 1 - mine, dim, keepdims=False)
    got = exchange(send, axis_name, mask)
    return (keep.astype(jnp.float32) + got.astype(jnp.float32)).astype(jnp.bfloat16)


def masks_of(axis_name):
    count = lax.axis_size(axis_name)
    return [1 << bit for bit in range(count.bit_length() - 1)]


def share_of(grads, high_first):
    taps, channels, width = grads.shape
    owners = lax.axis_size("frame")
    rows = channels // owners
    part = grads.astype(jnp.bfloat16).reshape(taps, owners, rows, width)
    part = jnp.swapaxes(part, 0, 1).reshape(owners, taps * rows, width)
    dp_masks = masks_of("dp")
    spare = -(taps * rows) % lax.axis_size("dp")
    if spare:
        part = jnp.pad(part, ((0, 0), (0, spare), (0, 0)))
    lead = part.shape[0]
    part = halve(part.reshape(lead, 2, -1, width), 1, "dp", dp_masks[0])
    frame_masks = masks_of("frame")
    for mask in reversed(frame_masks) if high_first else frame_masks:
        lead = part.shape[0] // 2
        if high_first:
            part = halve(part.reshape((2, lead) + part.shape[1:]), 0, "frame", mask)
        else:
            part = halve(part.reshape((lead, 2) + part.shape[1:]), 1, "frame", mask)
    part = part[0]
    for mask in dp_masks[1:]:
        part = halve(part.reshape(2, -1, width), 0, "dp", mask)
    return part


def whole_of(part, taps, rows):
    for mask in reversed(masks_of("dp")):
        got = exchange(part, "dp", mask)
        upper = jnp.bitwise_and(lax.axis_index("dp") // mask, 1) == 1
        part = jnp.concatenate([jnp.where(upper, got, part), jnp.where(upper, part, got)], axis=0)
    return part[: taps * rows].reshape(taps, rows, -1).astype(jnp.float32)


def owned_step(spatial_weight, temporal_weight, spatial_part, temporal_part, factor):
    rows_each = spatial_part.shape[1]
    cols_each = spatial_part.shape[2]
    row_start = lax.axis_index("frame") * rows_each
    spatial_here = lax.dynamic_slice(spatial_weight, (0, row_start, 0), (9, rows_each, cols_each))
    temporal_here = lax.dynamic_slice(temporal_weight, (0, row_start, 0), (3, rows_each, cols_each))
    new_spatial = spatial_here.astype(jnp.float32) - factor * spatial_part
    new_temporal = temporal_here.astype(jnp.float32) - factor * temporal_part
    return (new_spatial, new_temporal)


def on_device(latents, cotangent, timesteps, spatial_weight, temporal_weight):
    channels = latents.shape[3]
    pixels = latents.shape[2]
    frames = lax.axis_size("frame")
    cot_here = cotangent.reshape(pixels, channels)
    cot_next = lax.ppermute(cot_here, "frame", [(i, i - 1) for i in range(1, frames)])
    cot_prev = lax.ppermute(cot_here, "frame", [(i, i + 1) for i in range(frames - 1)])
    shifts = embed(timesteps, channels)
    activated = jax.nn.silu(latents.astype(jnp.float32) + shifts[:, None, None, :]).astype(
        jnp.bfloat16
    )
    columns = unfold(activated.reshape(-1, pixels, channels), SLAB, WIDTH).reshape(-1, 9 * channels)
    pre_act = jnp.dot(
        columns, spatial_weight.reshape(9 * channels, channels), preferred_element_type=jnp.float32
    )
    gated = jax.nn.silu(pre_act).astype(jnp.bfloat16)
    shifted = (cot_next, cot_here, cot_prev)
    grad_gated = jnp.zeros((pixels, channels), jnp.float32)
    for offset in range(3):
        grad_gated = grad_gated + jnp.einsum(
            "rd,cd->rc", shifted[offset], temporal_weight[offset], preferred_element_type=jnp.float32
        )
    grad_pre = (
        grad_gated.astype(jnp.bfloat16).astype(jnp.float32) * silu_slope(pre_act)
    ).astype(jnp.bfloat16)
    temporal_grad = jnp.stack(
        [
            jnp.einsum("rc,rd->cd", gated, cot, preferred_element_type=jnp.float32)
            for cot in shifted
        ]
    )
    shares = [share_of(temporal_grad, False)]
    for row_off in range(3):
        block = columns[:, 3 * row_off * channels : 3 * (row_off + 1) * channels]
        grads = jnp.einsum("rk,rc->kc", block, grad_pre, preferred_element_type=jnp.float32)
        shares.append(share_of(grads.reshape(3, channels, channels), row_off % 2 == 0))
    local = sum(jnp.sum(jnp.square(share.astype(jnp.float32))) for share in shares)
    squares = lax.psum(local, ("dp", "frame"))
    temporal_part, *spatial_parts = [whole_of(share, 3, channels // frames) for share in shares]
    spatial_part = jnp.concatenate(spatial_parts, axis=0)
    factor = clip_factor(squares, channels)
    return owned_step(spatial_weight, temporal_weight, spatial_part, temporal_part, factor)


def solution(mesh):
    in_specs = (P("dp", "frame", None, None), P("dp", "frame", None, None), P("dp"), P(), P())
    out_specs = (P(None, "frame", None), P(None, "frame", None))
    return jax.shard_map(
        on_device, mesh=mesh, in_specs=in_specs, out_specs=out_specs, check_vma=False
    )
```
